32 devices in a mesh: role: 4 (over z), seq: 2 (over y), tp: 4 (over x, core).
Axes of the slice: x: 2, y: 2, z: 4, core: 2. Of those that a mesh axis runs over, the one named last changes fastest.
Arguments:
- teacher_rows: bfloat16 [4, 1024, 8192], P('role', 'seq', 'tp'), may hold values from -16 to 16
- teacher_gain: float32 [8192], P('tp'), may hold values from 0.5 to 1.5
- proj: bfloat16 [8192, 4096], P('tp', 'seq'), may hold values from -0.0625 to 0.0625
- streams: bfloat16 [4, 1024, 4, 4096], P('role', 'seq', None, 'tp'), may hold values from -5 to 5
- hc_read: float32 [4], replicated, may hold values from 0.5 to 1.5
- hc_mix: float32 [4, 4], replicated, may hold values from -3 to 3
- hc_write: float32 [4], replicated, may hold values from 0.5 to 1.5
- norm_gain: float32 [4096], P('tp'), may hold values from 0.5 to 1.5
- w_query: bfloat16 [4096, 4096], P('seq', 'tp'), may hold values from -0.09375 to 0.09375
- w_kv: bfloat16 [4096, 2048], P('tp'), may hold values from -0.09375 to 0.09375
- w_out: bfloat16 [4096, 4096], P('tp', 'seq'), may hold values from -0.09375 to 0.09375
Outputs:
- grad_streams: bfloat16 [4, 1024, 4, 4096], P('role', 'seq', None, 'tp')
- loss_value: float32 [], replicated
The draws below stay inside these ranges and needn't reach their ends.
All inputs are finite; a program needn't handle non-finite values.
Results may differ from the reference program's by a relative error of at most 0.024.
Values may be sent and summed in bfloat16 or wider, within the bound.
A program may use at most 192 MiB of HBM per device.

```python
import jax
import jax.numpy as jnp
from jax import lax

DT = 8192
DS = 4096
HEADS = 32
KVH = 8
HD = 128
NS = 4
LEN = 1024
BATCH = 4
N_ROLE = 4
N_SEQ = 2
N_TP = 4


def draw_teacher_rows(key, part):
    key = jax.random.fold_in(key, 11)
    first_key, second_key = jax.random.split(key, 2)
    place = jnp.arange(DT, dtype=jnp.float32) / (DT - 1)
    rough = jax.random.uniform(second_key, (DT,), jnp.float32, 0.7, 1.3)
    column = jnp.exp(jnp.log(0.3) + place * jnp.log(10.0)) * rough
    base = jax.random.truncated_normal(first_key, -4.0, 4.0, (BATCH, LEN, DT), jnp.float32)
    return (base * column[None, None, :]).astype(jnp.bfloat16)


def draw_streams(key, part):
    key = jax.random.fold_in(key, 23)
    member = jnp.arange(BATCH, dtype=jnp.float32) / max(BATCH - 1, 1)
    level = jnp.exp(jnp.log(0.3) + member * jnp.log(4.0))
    base = jax.random.truncated_normal(key, -4.0, 4.0, (BATCH, LEN, NS, DS), jnp.float32)
    return (base * level[:, None, None, None]).astype(jnp.bfloat16)


def shard_levels(own_key, extent, cuts, least, high):
    factor_of, own = 1.0, jax.random.fold_in(own_key, 6)
    for axis_at, shards_of in cuts:
        steps = jnp.exp(jax.random.uniform(jax.random.fold_in(own, axis_at), (shards_of,), jnp.float32, least / len(cuts), high / len(cuts)))
        factor_of = factor_of * jnp.repeat(steps, extent[axis_at] // shards_of).reshape([-1 if axis == axis_at else 1 for axis in range(len(extent))])
    return factor_of


def centred(stream_key, shape, spread, bound, shards=(), held_as=jnp.bfloat16):
    factor_of = shard_levels(stream_key, shape, shards, -0.22, 0.18) if shards else 1.0
    entries = jax.random.normal(stream_key, shape, jnp.float32) * spread * factor_of
    return jnp.minimum(jnp.maximum(entries, -bound), bound).astype(held_as)


def setup_inputs(seed: int = 0) -> dict:
    key_of = jax.random.split(jax.random.key(seed), 12)
    return {
        "teacher_rows": draw_teacher_rows(jax.random.fold_in(key_of[11], 71), 0),
        "teacher_gain": jnp.clip(1.0 + 0.1 * jax.random.normal(key_of[1], (DT,), jnp.float32), 0.5, 1.5),
        "proj": centred(key_of[2], (DT, DS), DT ** -0.5, 0.0625, ((0, 4), (1, 2))),
        "streams": draw_streams(jax.random.fold_in(key_of[11], 71), 0),
        "hc_read": jnp.clip(jax.random.uniform(key_of[4], (NS,), jnp.float32, 0.5, 1.5), 0.5, 1.5),
        "hc_mix": centred(key_of[5], (NS, NS), 0.5, 3.0, (), jnp.float32),
        "hc_write": jnp.clip(jax.random.uniform(key_of[6], (NS,), jnp.float32, 0.5, 1.5), 0.5, 1.5),
        "norm_gain": jnp.clip(1.0 + 0.1 * jax.random.normal(key_of[7], (DS,), jnp.float32), 0.5, 1.5),
        "w_query": centred(key_of[8], (DS, HEADS * HD), DS ** -0.5, 0.09375, ((0, 2), (1, 4))),
        "w_kv": centred(key_of[9], (DS, 2 * KVH * HD), DS ** -0.5, 0.09375, ((0, 4),)),
        "w_out": centred(key_of[10], (HEADS * HD, DS), (HEADS * HD) ** -0.5, 0.09375, ((0, 4), (1, 2))),
    }


epsilon = 1e-05

def rounded(values):
    return lax.optimization_barrier(values.astype(jnp.bfloat16)).astype(jnp.float32)

def reference(teacher_rows, teacher_gain, proj, streams, hc_read, hc_mix, hc_write, norm_gain, w_query, w_kv, w_out):
    f32 = jnp.float32
    high = lax.Precision.HIGHEST
    heads_dev = HEADS // N_TP
    group = HEADS // KVH
    ratio = max(1, group // heads_dev)
    loc = LEN // N_SEQ
    dt_block = DT // N_TP
    ds_block = DS // N_TP
    scale = HD ** (-0.5)
    carry = lax.optimization_barrier(jnp.sum(hc_mix, axis=0))
    write = jnp.sum(hc_write)
    places = jnp.arange(LEN)
    allowed = places[None, :] <= places[:, None]
    eye_tp = jnp.eye(N_TP, dtype=f32)
    grads = []
    loss_total = jnp.zeros((), f32)
    for member in range(N_ROLE):
        teacher = teacher_rows[member].astype(f32)
        inv_t = lax.rsqrt(lax.optimization_barrier(jnp.mean(teacher * teacher, axis=1)) + epsilon)
        normed_t = (teacher * inv_t[:, None] * teacher_gain[None, :]).astype(jnp.bfloat16)
        parts = jnp.einsum('lnd,nde->nle', normed_t.reshape(LEN, N_TP, dt_block).astype(f32), proj.reshape(N_TP, dt_block, DS).astype(f32), precision=high)
        target = lax.optimization_barrier(jnp.sum(rounded(parts), axis=0))
        hidden = streams[member].astype(f32)
        mixed_in = lax.optimization_barrier(jnp.sum(hidden * hc_read[None, :, None], axis=1))
        inv_rms = lax.rsqrt(lax.optimization_barrier(jnp.mean(mixed_in ** 2, axis=1)) + epsilon)
        normed_s = (mixed_in * inv_rms[:, None] * norm_gain[None, :]).astype(jnp.bfloat16)
        query = jnp.dot(normed_s, w_query, preferred_element_type=f32).astype(jnp.bfloat16)
        kv_parts = jnp.einsum('lnd,nde->nle', normed_s.reshape(LEN, N_TP, ds_block).astype(f32), w_kv.reshape(N_TP, ds_block, 2 * KVH * HD).astype(f32), precision=high)
        kv_all = lax.optimization_barrier(jnp.sum(rounded(kv_parts), axis=0)).astype(jnp.bfloat16)
        query4 = query.reshape(LEN, KVH, group, HD).astype(f32)
        keys = kv_all[:, :KVH * HD].reshape(LEN, KVH, HD).astype(f32)
        values = kv_all[:, KVH * HD:].reshape(LEN, KVH, HD).astype(f32)
        scores = jnp.einsum('qgjd,kgd->gjqk', query4, keys, precision=high) * scale
        scores = jnp.where(allowed, scores, -1e+30)
        expo = jnp.exp(scores)
        probs = expo / lax.optimization_barrier(jnp.sum(expo, axis=-1, keepdims=True))
        probs_low = rounded(probs)
        attended = jnp.einsum('gjqk,kgd->qgjd', probs_low, values, precision=high).astype(jnp.bfloat16)
        attended = attended.reshape(LEN, HEADS * HD)
        out_parts = jnp.einsum('lnh,nhe->nle', attended.reshape(LEN, N_TP, heads_dev * HD).astype(f32), w_out.reshape(N_TP, heads_dev * HD, DS).astype(f32), precision=high)
        layer_out = lax.optimization_barrier(jnp.sum(rounded(out_parts), axis=0))
        student = lax.optimization_barrier(jnp.sum(hidden * carry[None, :, None], axis=1)) + write * layer_out
        error = student - target
        loss_total = loss_total + jnp.sum(error * error)
        grad_out = (write * error).astype(jnp.bfloat16)
        grad_att = lax.dot_general(grad_out, w_out, (((1,), (1,)), ((), ())), preferred_element_type=f32).astype(jnp.bfloat16)
        grad4 = grad_att.reshape(LEN, KVH, group, HD).astype(f32)
        att4 = attended.reshape(LEN, KVH, group, HD).astype(f32)
        grad_probs = jnp.einsum('qgjd,kgd->gjqk', grad4, values, precision=high)
        delta = jnp.einsum('qgjd,qgjd->gjq', grad4, att4, precision=high)
        grad_scores = rounded(probs * (grad_probs - delta[..., None]))
        grad_query = (jnp.einsum('gjqk,kgd->qgjd', grad_scores, keys, precision=high) * scale).astype(jnp.bfloat16)
        grad_query = grad_query.reshape(LEN, HEADS * HD)
        scores5 = grad_scores.reshape(KVH, group, N_SEQ, loc, LEN)
        probs5 = probs_low.reshape(KVH, group, N_SEQ, loc, LEN)
        query5 = query4.reshape(N_SEQ, loc, KVH, group, HD)
        grad5 = grad4.reshape(N_SEQ, loc, KVH, group, HD)
        key_cont = jnp.einsum('gjsqk,sqgjd->gjskd', scores5, query5, precision=high) * scale
        val_cont = jnp.einsum('gjsqk,sqgjd->gjskd', probs5, grad5, precision=high)
        key_cont = lax.optimization_barrier(jnp.sum(key_cont.reshape(KVH, ratio, group // ratio, N_SEQ, LEN, HD), axis=2))
        val_cont = lax.optimization_barrier(jnp.sum(val_cont.reshape(KVH, ratio, group // ratio, N_SEQ, LEN, HD), axis=2))
        key_group = rounded(lax.optimization_barrier(jnp.sum(rounded(key_cont), axis=2)))
        val_group = rounded(lax.optimization_barrier(jnp.sum(rounded(val_cont), axis=2)))
        key_grad = lax.optimization_barrier(jnp.sum(key_group, axis=1)).astype(jnp.bfloat16)
        val_grad = lax.optimization_barrier(jnp.sum(val_group, axis=1)).astype(jnp.bfloat16)
        grad_kv = jnp.concatenate([key_grad.transpose(1, 0, 2).reshape(LEN, KVH * HD), val_grad.transpose(1, 0, 2).reshape(LEN, KVH * HD)], axis=1)
        query_parts = jnp.einsum('lnh,dnh->nld', grad_query.reshape(LEN, N_TP, heads_dev * HD).astype(f32), w_query.reshape(DS, N_TP, heads_dev * HD).astype(f32), precision=high)
        kv_side = lax.dot_general(grad_kv, w_kv, (((1,), (1,)), ((), ())), preferred_element_type=f32)
        terms = query_parts.reshape(N_TP, LEN, N_TP, ds_block) + eye_tp[:, None, :, None] * kv_side.reshape(LEN, N_TP, ds_block)[None]
        grad_normed = lax.optimization_barrier(jnp.sum(rounded(terms), axis=0)).reshape(LEN, DS)
        scaled = grad_normed * norm_gain[None, :]
        inner = lax.optimization_barrier(jnp.mean(scaled * mixed_in, axis=1))
        grad_in = inv_rms[:, None] * scaled - mixed_in * (inv_rms ** 3 * inner)[:, None]
        grad_streams = carry[None, :, None] * error[:, None, :] + hc_read[None, :, None] * grad_in[:, None, :]
        grads.append(grad_streams.astype(jnp.bfloat16))
    return (jnp.stack(grads), loss_total / (N_ROLE * LEN * DS))
```

```python
import jax
import jax.numpy as jnp
from jax import lax
from jax.experimental import pallas as pl
from jax.experimental.pallas import tpu as pltpu
from jax.sharding import PartitionSpec as P

HEADS = 32
KVH = 8
HD = 128


epsilon = 1e-05


def per_device_rows(
    teacher_rows,
    teacher_gain,
    proj,
    streams,
    hc_read,
    hc_mix,
    hc_write,
    norm_gain,
    w_query,
    w_kv,
    w_out,
):
    f32 = jnp.float32
    bf16 = jnp.bfloat16
    n_tp = lax.axis_size("tp")
    tp_index = lax.axis_index("tp")
    seq_index = lax.axis_index("seq")
    teacher = teacher_rows[0].astype(f32)
    hidden = streams[0].astype(f32)
    mixed_in = jnp.sum(hidden * hc_read[None, :, None], axis=1)
    feat_block = mixed_in.shape[1]
    teacher_sq, student_sq = lax.psum(
        (jnp.sum(teacher * teacher, axis=1), jnp.sum(mixed_in * mixed_in, axis=1)), "tp"
    )
    inv_t = lax.rsqrt(teacher_sq / (teacher.shape[1] * n_tp) + epsilon)
    normed_t = (teacher * inv_t[:, None] * teacher_gain[None, :]).astype(bf16)
    local_len = normed_t.shape[0]
    proj_full = lax.all_gather(proj, "seq", axis=1, tiled=True)
    target_term = jnp.dot(normed_t, proj_full, preferred_element_type=f32)
    target = lax.psum_scatter(
        target_term.astype(jnp.bfloat16), "tp", scatter_dimension=1, tiled=True
    ).astype(jnp.float32)
    inv_rms = lax.rsqrt(student_sq / (feat_block * n_tp) + epsilon)
    normed_s = (mixed_in * inv_rms[:, None] * norm_gain[None, :]).astype(bf16)
    heads_dev = w_query.shape[1] // HD
    group = HEADS // KVH
    kv_dev = max(1, heads_dev // group)
    per_kv = heads_dev // kv_dev
    ratio = max(1, group // heads_dev)
    first = tp_index * heads_dev // group
    query_full = lax.all_gather(w_query, "seq", axis=0, tiled=True)
    kv_part = jnp.dot(normed_s, w_kv, preferred_element_type=f32)
    kv_all = lax.psum(kv_part.astype(jnp.bfloat16), "tp").astype(jnp.float32).astype(bf16)
    keys_own = lax.dynamic_slice_in_dim(kv_all, first * HD, kv_dev * HD, 1)
    vals_own = lax.dynamic_slice_in_dim(kv_all, (KVH + first) * HD, kv_dev * HD, 1)
    rows_full = lax.all_gather(normed_s, "tp", axis=1, tiled=True)
    query = jnp.dot(rows_full, query_full, preferred_element_type=f32).astype(bf16)
    keys_all, vals_all = (
        lax.all_gather(keys_own, "seq", axis=0, tiled=True),
        lax.all_gather(vals_own, "seq", axis=0, tiled=True),
    )
    whole_len = keys_all.shape[0]
    scale = HD ** (-0.5)
    query4 = query.reshape(local_len, kv_dev, per_kv, HD)
    keys3 = keys_all.reshape(whole_len, kv_dev, HD)
    vals3 = vals_all.reshape(whole_len, kv_dev, HD)
    scores = jnp.einsum("qgjd,kgd->gjqk", query4, keys3, preferred_element_type=f32) * scale
    query_pos = seq_index * local_len + lax.iota(jnp.int32, local_len)
    key_pos = lax.iota(jnp.int32, whole_len)
    allowed = key_pos[None, :] <= query_pos[:, None]
    scores = jnp.where(allowed, scores, -1e30)
    expo = jnp.exp(scores)
    probs = expo / jnp.sum(expo, axis=-1, keepdims=True)
    probs_low = probs.astype(bf16)
    attended = jnp.einsum("gjqk,kgd->qgjd", probs_low, vals3, preferred_element_type=f32).astype(
        bf16
    )
    attended = attended.reshape(local_len, heads_dev * HD)
    out_full = lax.all_gather(w_out, "seq", axis=1, tiled=True)
    out_term = jnp.dot(attended, out_full, preferred_element_type=f32)
    layer_out = lax.psum_scatter(
        out_term.astype(jnp.bfloat16), "tp", scatter_dimension=1, tiled=True
    ).astype(jnp.float32)
    carry = jnp.sum(hc_mix, axis=0)
    write = jnp.sum(hc_write)
    student = jnp.sum(hidden * carry[None, :, None], axis=1) + write * layer_out
    error = student - target
    loss_total = lax.psum(jnp.sum(error * error), ("role", "seq", "tp"))
    loss_value = loss_total / (lax.axis_size("role") * whole_len * feat_block * n_tp)
    grad_out = (write * error).astype(bf16)
    grad_full = lax.all_gather(grad_out, "tp", axis=1, tiled=True)
    grad_att = lax.dot_general(
        grad_full, out_full, (((1,), (1,)), ((), ())), preferred_element_type=f32
    ).astype(bf16)
    grad4 = grad_att.reshape(local_len, kv_dev, per_kv, HD)
    att4 = attended.reshape(local_len, kv_dev, per_kv, HD)
    grad_probs = jnp.einsum("qgjd,kgd->gjqk", grad4, vals3, preferred_element_type=f32)
    delta = jnp.einsum("qgjd,qgjd->gjq", grad4, att4, preferred_element_type=f32)
    grad_scores = (probs * (grad_probs - delta[..., None])).astype(bf16)
    grad_query = (
        jnp.einsum("gjqk,kgd->qgjd", grad_scores, keys3, preferred_element_type=f32) * scale
    ).astype(bf16)
    grad_query = grad_query.reshape(local_len, heads_dev * HD)
    grad_keys = (
        jnp.einsum("gjqk,qgjd->kgd", grad_scores, query4, preferred_element_type=f32) * scale
    )
    grad_vals = jnp.einsum("gjqk,qgjd->kgd", probs_low, grad4, preferred_element_type=f32)
    key_sum, val_sum = (
        lax.psum_scatter(
            grad_keys.reshape(whole_len, kv_dev * HD).astype(jnp.bfloat16),
            "seq",
            scatter_dimension=0,
            tiled=True,
        ).astype(jnp.float32),
        lax.psum_scatter(
            grad_vals.reshape(whole_len, kv_dev * HD).astype(jnp.bfloat16),
            "seq",
            scatter_dimension=0,
            tiled=True,
        ).astype(jnp.float32),
    )
    key_parts, val_parts = (
        lax.all_gather(key_sum.astype(bf16), "tp", axis=1, tiled=True),
        lax.all_gather(val_sum.astype(bf16), "tp", axis=1, tiled=True),
    )
    key_grad = jnp.sum(
        key_parts.astype(f32).reshape(local_len, n_tp // ratio, ratio, kv_dev * HD), axis=2
    )
    val_grad = jnp.sum(
        val_parts.astype(f32).reshape(local_len, n_tp // ratio, ratio, kv_dev * HD), axis=2
    )
    grad_kv = jnp.concatenate(
        [key_grad.reshape(local_len, KVH * HD), val_grad.reshape(local_len, KVH * HD)], axis=1
    ).astype(bf16)
    base = lax.dot_general(
        grad_query, query_full, (((1,), (1,)), ((), ())), preferred_element_type=f32
    )
    side = lax.dot_general(grad_kv, w_kv, (((1,), (1,)), ((), ())), preferred_element_type=f32)
    current = lax.dynamic_slice_in_dim(base, tp_index * feat_block, feat_block, 1)
    input_term = lax.dynamic_update_slice_in_dim(base, current + side, tp_index * feat_block, 1)
    grad_normed = lax.psum_scatter(
        input_term.astype(jnp.bfloat16), "tp", scatter_dimension=1, tiled=True
    ).astype(jnp.float32)
    scaled = grad_normed * norm_gain[None, :]
    inner_part = jnp.sum(scaled * mixed_in, axis=1)
    inner = lax.psum(inner_part, "tp") / (feat_block * n_tp)
    grad_in = inv_rms[:, None] * scaled - mixed_in * (inv_rms**3 * inner)[:, None]
    grad_streams = (
        carry[None, :, None] * error[:, None, :] + hc_read[None, :, None] * grad_in[:, None, :]
    )
    return (grad_streams.astype(bf16)[None], loss_value)


BLOCK = 256


def dot_rows(left, right):
    return lax.dot_general(left, right, (((1,), (1,)), ((), ())), preferred_element_type=jnp.float32)


def dot_cols(left, right):
    return lax.dot_general(left, right, (((0,), (0,)), ((), ())), preferred_element_type=jnp.float32)


def block_probs(query, keys, start):
    rows, width = query.shape[0], keys.shape[0]
    expo = jnp.exp(dot_rows(query, keys) * HD ** (-0.5))
    row = start + lax.broadcasted_iota(jnp.int32, (rows, width), 0)
    col = lax.broadcasted_iota(jnp.int32, (rows, width), 1)
    expo = jnp.where(col <= row, expo, 0.0)
    return expo / jnp.sum(expo, axis=1, keepdims=True)


def attend_kernel(query_ref, keys_ref, vals_ref, out_ref):
    for start in range(0, query_ref.shape[0], BLOCK):
        stop = start + BLOCK
        probs = block_probs(query_ref[start:stop, :], keys_ref[:stop, :], start)
        out_ref[start:stop, :] = jnp.dot(
            probs.astype(jnp.bfloat16), vals_ref[:stop, :], preferred_element_type=jnp.float32
        ).astype(jnp.bfloat16)


def attend(query, keys, vals):
    length, width = query.shape
    heads = pl.BlockSpec((length, HD), lambda h: (0, h))
    whole = pl.BlockSpec((length, HD), lambda h: (0, 0))
    return pl.pallas_call(
        attend_kernel,
        grid=(width // HD,),
        in_specs=[heads, whole, whole],
        out_specs=heads,
        out_shape=jax.ShapeDtypeStruct((length, width), jnp.bfloat16),
        compiler_params=pltpu.CompilerParams(vmem_limit_bytes=32 * 2**20),
        cost_estimate=pl.CostEstimate(
            flops=length * length * width * 3, bytes_accessed=length * width * 4, transcendentals=0
        ),
        name="attend",
    )(query, keys, vals)


def attend_grad_kernel(query_ref, keys_ref, vals_ref, att_ref, grad_ref, gq_ref, gk_ref, gv_ref):
    @pl.when(pl.program_id(0) == 0)
    def _():
        gk_ref[...] = jnp.zeros_like(gk_ref)
        gv_ref[...] = jnp.zeros_like(gv_ref)

    scale = HD ** (-0.5)
    for start in range(0, query_ref.shape[0], BLOCK):
        stop = start + BLOCK
        query = query_ref[start:stop, :]
        keys = keys_ref[:stop, :]
        grad = grad_ref[start:stop, :]
        probs = block_probs(query, keys, start)
        delta = jnp.sum(
            grad.astype(jnp.float32) * att_ref[start:stop, :].astype(jnp.float32),
            axis=1,
            keepdims=True,
        )
        grad_scores = (probs * (dot_rows(grad, vals_ref[:stop, :]) - delta)).astype(jnp.bfloat16)
        gq_ref[start:stop, :] = (
            jnp.dot(grad_scores, keys, preferred_element_type=jnp.float32) * scale
        ).astype(jnp.bfloat16)
        gk_ref[:stop, :] += dot_cols(grad_scores, query) * scale
        gv_ref[:stop, :] += dot_cols(probs.astype(jnp.bfloat16), grad)


def attend_grad(query, keys, vals, att, grad):
    length, width = query.shape
    heads = pl.BlockSpec((length, HD), lambda h: (0, h))
    whole = pl.BlockSpec((length, HD), lambda h: (0, 0))
    kv_shape = jax.ShapeDtypeStruct((length, HD), jnp.float32)
    return pl.pallas_call(
        attend_grad_kernel,
        grid=(width // HD,),
        in_specs=[heads, whole, whole, heads, heads],
        out_specs=[heads, whole, whole],
        out_shape=[jax.ShapeDtypeStruct((length, width), jnp.bfloat16), kv_shape, kv_shape],
        compiler_params=pltpu.CompilerParams(vmem_limit_bytes=32 * 2**20),
        cost_estimate=pl.CostEstimate(
            flops=length * length * width * 6, bytes_accessed=length * width * 8, transcendentals=0
        ),
        name="attend_grad",
    )(query, keys, vals, att, grad)


def per_device_heads(
    teacher_rows,
    teacher_gain,
    proj,
    streams,
    hc_read,
    hc_mix,
    hc_write,
    norm_gain,
    w_query,
    w_kv,
    w_out,
):
    f32 = jnp.float32
    bf16 = jnp.bfloat16
    n_seq = lax.axis_size("seq")
    n_tp = lax.axis_size("tp")
    s = lax.axis_index("seq")
    per = n_tp // n_seq
    length = teacher_rows.shape[1]
    whole_len = length * n_seq
    feat = streams.shape[3]
    features = feat * n_tp
    swap_pairs = [(0, 1), (1, 0)]
    turn_pairs = [
        (a * n_tp + t, (t // per) * n_tp + a * per + t % per)
        for a in range(n_seq)
        for t in range(n_tp)
    ]

    def swap(array):
        return lax.ppermute(array, "seq", swap_pairs)

    def turn(array):
        return lax.ppermute(array, ("seq", "tp"), turn_pairs)

    def half(array, index, axis):
        size = array.shape[axis] // n_seq
        return lax.dynamic_slice_in_dim(array, index * size, size, axis)

    def gather_turned(array):
        parts = lax.all_gather(array, "tp", axis=0)
        parts = parts.reshape(n_seq, per, length, feat).transpose(0, 2, 1, 3)
        return parts.reshape(whole_len, per * feat)

    def scatter_turned(term):
        parts = term.reshape(n_seq, length, per, feat).transpose(0, 2, 1, 3)
        parts = parts.reshape(n_tp, length, feat)
        return lax.psum_scatter(parts, "tp", scatter_dimension=0, tiled=False)

    def by_seq(own, other):
        return jnp.where(s == 0, own, other), jnp.where(s == 0, other, own)

    hidden = streams[0].astype(f32)
    mixed_in = jnp.sum(hidden * hc_read[None, :, None], axis=1)
    scaled_in = (mixed_in * norm_gain[None, :]).astype(bf16)
    turned_in = turn(scaled_in)
    rows = gather_turned(turned_in)

    teacher = teacher_rows[0]
    teacher_f = teacher.astype(f32)
    teacher_gained = (teacher_f * teacher_gain[None, :]).astype(bf16)
    sums = jnp.stack([jnp.sum(mixed_in * mixed_in, axis=1), jnp.sum(teacher_f * teacher_f, axis=1)])
    placed_sums = lax.dynamic_update_slice_in_dim(
        jnp.zeros((2, whole_len), f32), sums, s * length, 1
    )
    sums_all = lax.psum(placed_sums, ("seq", "tp"))
    inv_rms_all = lax.rsqrt(sums_all[0] / features + epsilon)
    inv_t_all = lax.rsqrt(sums_all[1] / (teacher.shape[1] * n_tp) + epsilon)
    inv_rms = lax.dynamic_slice_in_dim(inv_rms_all, s * length, length, 0)

    kv_part = jnp.dot(scaled_in, w_kv, preferred_element_type=f32)
    kv_heads = KVH // n_tp
    kv_part = kv_part.astype(bf16).reshape(length, 2, n_tp, kv_heads * HD).transpose(2, 0, 1, 3)
    kv_sum = lax.psum_scatter(kv_part, "tp", scatter_dimension=0, tiled=False)
    kv_sum = (kv_sum.astype(f32) * inv_rms[:, None, None]).astype(bf16)
    kv_own = half(kv_sum, s, 2)
    kv_other = swap(half(kv_sum, 1 - s, 2))
    kv_low, kv_high = by_seq(kv_own, kv_other)
    kv = jnp.concatenate([kv_low, kv_high], axis=0)
    keys, vals = kv[:, 0], kv[:, 1]

    query_far = jnp.dot(rows, half(w_query, 1 - s, 1), preferred_element_type=f32).astype(bf16)
    query_got = swap(query_far)
    query_own = jnp.dot(rows, half(w_query, s, 1), preferred_element_type=f32)
    query = ((query_own + query_got.astype(f32)) * inv_rms_all[:, None]).astype(bf16)

    teacher_got = swap(teacher_gained)
    teacher_low, teacher_high = by_seq(teacher_gained, teacher_got)
    target_term = jnp.dot(
        jnp.concatenate([teacher_low, teacher_high], axis=0), proj, preferred_element_type=f32
    )
    target_term = target_term * inv_t_all[:, None]

    carry = jnp.sum(hc_mix, axis=0)
    write = jnp.sum(hc_write)
    carried = turn(jnp.sum(hidden * carry[None, :, None], axis=1).astype(bf16))

    attended = attend(query, keys, vals)
    attended_got = swap(attended)
    out_term = jnp.dot(attended, half(w_out, s, 0), preferred_element_type=f32)
    out_term = out_term + jnp.dot(
        attended_got, half(w_out, 1 - s, 0), preferred_element_type=f32
    )
    term = (write * out_term - target_term).astype(bf16)
    error = carried.astype(f32) + scatter_turned(term).astype(f32)
    loss_total = lax.psum(jnp.sum(error * error), ("role", "seq", "tp"))
    loss_value = loss_total / (lax.axis_size("role") * whole_len * features)
    grad_full = gather_turned((write * error).astype(bf16))
    error_back = turn(error.astype(bf16))

    grad_far = dot_rows(grad_full, half(w_out, 1 - s, 0)).astype(bf16)
    grad_got = swap(grad_far)
    grad_own = dot_rows(grad_full, half(w_out, s, 0))
    grad_att = (grad_own + grad_got.astype(f32)).astype(bf16)

    grad_query, grad_keys, grad_vals = attend_grad(query, keys, vals, attended, grad_att)
    grad_query_got = swap(grad_query)
    grad_kv = jnp.stack([grad_keys, grad_vals], axis=1).astype(bf16)
    inner_part = jnp.sum(grad_query.astype(f32) * query.astype(f32), axis=1) + jnp.sum(
        grad_kv.astype(f32) * kv.astype(f32), axis=(1, 2)
    )
    inner_all = lax.psum(inner_part, ("seq", "tp")) / features
    inner = lax.dynamic_slice_in_dim(inner_all, s * length, length, 0)

    base = dot_rows(grad_query, half(w_query, s, 1))
    base = base + dot_rows(grad_query_got, half(w_query, 1 - s, 1))
    base_sum = turn(scatter_turned(base.astype(bf16)))

    grad_kv_got = swap(half(grad_kv, 1 - s, 0))
    grad_kv_low, grad_kv_high = by_seq(half(grad_kv, s, 0), grad_kv_got)
    grad_kv_own = jnp.concatenate([grad_kv_low, grad_kv_high], axis=2)
    grad_kv_all = lax.all_gather(grad_kv_own, "tp", axis=2, tiled=True).reshape(length, -1)
    side = dot_rows(grad_kv_all, w_kv)

    scaled = (base_sum.astype(f32) + side) * norm_gain[None, :]
    grad_in = inv_rms[:, None] * scaled - mixed_in * (inv_rms**2 * inner)[:, None]
    grad_streams = (
        carry[None, :, None] * error_back.astype(f32)[:, None, :]
        + hc_read[None, :, None] * grad_in[:, None, :]
    )
    return (grad_streams.astype(bf16)[None], loss_value)


def solution(mesh):
    placed = (
        P("role", "seq", "tp"),
        P("tp"),
        P("tp", "seq"),
        P("role", "seq", None, "tp"),
        P(),
        P(),
        P(),
        P("tp"),
        P("seq", "tp"),
        P("tp", None),
        P("tp", "seq"),
    )
    seq, tp = mesh.shape["seq"], mesh.shape["tp"]
    by_heads = seq == 2 and tp % seq == 0 and KVH % (seq * tp) == 0
    return jax.shard_map(
        per_device_heads if by_heads else per_device_rows,
        mesh=mesh,
        in_specs=placed,
        out_specs=(P("role", "seq", None, "tp"), P()),
        check_vma=False,
    )
```

```python
import jax
import jax.numpy as jnp
from jax import lax
from jax.experimental import pallas as pl
from jax.experimental.pallas import tpu as pltpu
from jax.sharding import PartitionSpec as P

HEADS = 32
KVH = 8
HD = 128


epsilon = 1e-05


def per_device_rows(
    teacher_rows,
    teacher_gain,
    proj,
    streams,
    hc_read,
    hc_mix,
    hc_write,
    norm_gain,
    w_query,
    w_kv,
    w_out,
):
    f32 = jnp.float32
    bf16 = jnp.bfloat16
    n_tp = lax.axis_size("tp")
    tp_index = lax.axis_index("tp")
    seq_index = lax.axis_index("seq")
    teacher = teacher_rows[0].astype(f32)
    hidden = streams[0].astype(f32)
    mixed_in = jnp.sum(hidden * hc_read[None, :, None], axis=1)
    feat_block = mixed_in.shape[1]
    teacher_sq, student_sq = lax.psum(
        (jnp.sum(teacher * teacher, axis=1), jnp.sum(mixed_in * mixed_in, axis=1)), "tp"
    )
    inv_t = lax.rsqrt(teacher_sq / (teacher.shape[1] * n_tp) + epsilon)
    normed_t = (teacher * inv_t[:, None] * teacher_gain[None, :]).astype(bf16)
    local_len = normed_t.shape[0]
    proj_full = lax.all_gather(proj, "seq", axis=1, tiled=True)
    target_term = jnp.dot(normed_t, proj_full, preferred_element_type=f32)
    target = lax.psum_scatter(
        target_term.astype(jnp.bfloat16), "tp", scatter_dimension=1, tiled=True
    ).astype(jnp.float32)
    inv_rms = lax.rsqrt(student_sq / (feat_block * n_tp) + epsilon)
    normed_s = (mixed_in * inv_rms[:, None] * norm_gain[None, :]).astype(bf16)
    heads_dev = w_query.shape[1] // HD
    group = HEADS // KVH
    kv_dev = max(1, heads_dev // group)
    per_kv = heads_dev // kv_dev
    ratio = max(1, group // heads_dev)
    first = tp_index * heads_dev // group
    query_full = lax.all_gather(w_query, "seq", axis=0, tiled=True)
    kv_part = jnp.dot(normed_s, w_kv, preferred_element_type=f32)
    kv_all = lax.psum(kv_part.astype(jnp.bfloat16), "tp").astype(jnp.float32).astype(bf16)
    keys_own = lax.dynamic_slice_in_dim(kv_all, first * HD, kv_dev * HD, 1)
    vals_own = lax.dynamic_slice_in_dim(kv_all, (KVH + first) * HD, kv_dev * HD, 1)
    rows_full = lax.all_gather(normed_s, "tp", axis=1, tiled=True)
    query = jnp.dot(rows_full, query_full, preferred_element_type=f32).astype(bf16)
    keys_all, vals_all = (
        lax.all_gather(keys_own, "seq", axis=0, tiled=True),
        lax.all_gather(vals_own, "seq", axis=0, tiled=True),
    )
    whole_len = keys_all.shape[0]
    scale = HD ** (-0.5)
    query4 = query.reshape(local_len, kv_dev, per_kv, HD)
    keys3 = keys_all.reshape(whole_len, kv_dev, HD)
    vals3 = vals_all.reshape(whole_len, kv_dev, HD)
    scores = jnp.einsum("qgjd,kgd->gjqk", query4, keys3, preferred_element_type=f32) * scale
    query_pos = seq_index * local_len + lax.iota(jnp.int32, local_len)
    key_pos = lax.iota(jnp.int32, whole_len)
    allowed = key_pos[None, :] <= query_pos[:, None]
    scores = jnp.where(allowed, scores, -1e30)
    expo = jnp.exp(scores)
    probs = expo / jnp.sum(expo, axis=-1, keepdims=True)
    probs_low = probs.astype(bf16)
    attended = jnp.einsum("gjqk,kgd->qgjd", probs_low, vals3, preferred_element_type=f32).astype(
        bf16
    )
    attended = attended.reshape(local_len, heads_dev * HD)
    out_full = lax.all_gather(w_out, "seq", axis=1, tiled=True)
    out_term = jnp.dot(attended, out_full, preferred_element_type=f32)
    layer_out = lax.psum_scatter(
        out_term.astype(jnp.bfloat16), "tp", scatter_dimension=1, tiled=True
    ).astype(jnp.float32)
    carry = jnp.sum(hc_mix, axis=0)
    write = jnp.sum(hc_write)
    student = jnp.sum(hidden * carry[None, :, None], axis=1) + write * layer_out
    error = student - target
    loss_total = lax.psum(jnp.sum(error * error), ("role", "seq", "tp"))
    loss_value = loss_total / (lax.axis_size("role") * whole_len * feat_block * n_tp)
    grad_out = (write * error).astype(bf16)
    grad_full = lax.all_gather(grad_out, "tp", axis=1, tiled=True)
    grad_att = lax.dot_general(
        grad_full, out_full, (((1,), (1,)), ((), ())), preferred_element_type=f32
    ).astype(bf16)
    grad4 = grad_att.reshape(local_len, kv_dev, per_kv, HD)
    att4 = attended.reshape(local_len, kv_dev, per_kv, HD)
    grad_probs = jnp.einsum("qgjd,kgd->gjqk", grad4, vals3, preferred_element_type=f32)
    delta = jnp.einsum("qgjd,qgjd->gjq", grad4, att4, preferred_element_type=f32)
    grad_scores = (probs * (grad_probs - delta[..., None])).astype(bf16)
    grad_query = (
        jnp.einsum("gjqk,kgd->qgjd", grad_scores, keys3, preferred_element_type=f32) * scale
    ).astype(bf16)
    grad_query = grad_query.reshape(local_len, heads_dev * HD)
    grad_keys = (
        jnp.einsum("gjqk,qgjd->kgd", grad_scores, query4, preferred_element_type=f32) * scale
    )
    grad_vals = jnp.einsum("gjqk,qgjd->kgd", probs_low, grad4, preferred_element_type=f32)
    key_sum, val_sum = (
        lax.psum_scatter(
            grad_keys.reshape(whole_len, kv_dev * HD).astype(jnp.bfloat16),
            "seq",
            scatter_dimension=0,
            tiled=True,
        ).astype(jnp.float32),
        lax.psum_scatter(
            grad_vals.reshape(whole_len, kv_dev * HD).astype(jnp.bfloat16),
            "seq",
            scatter_dimension=0,
            tiled=True,
        ).astype(jnp.float32),
    )
    key_parts, val_parts = (
        lax.all_gather(key_sum.astype(bf16), "tp", axis=1, tiled=True),
        lax.all_gather(val_sum.astype(bf16), "tp", axis=1, tiled=True),
    )
    key_grad = jnp.sum(
        key_parts.astype(f32).reshape(local_len, n_tp // ratio, ratio, kv_dev * HD), axis=2
    )
    val_grad = jnp.sum(
        val_parts.astype(f32).reshape(local_len, n_tp // ratio, ratio, kv_dev * HD), axis=2
    )
    grad_kv = jnp.concatenate(
        [key_grad.reshape(local_len, KVH * HD), val_grad.reshape(local_len, KVH * HD)], axis=1
    ).astype(bf16)
    base = lax.dot_general(
        grad_query, query_full, (((1,), (1,)), ((), ())), preferred_element_type=f32
    )
    side = lax.dot_general(grad_kv, w_kv, (((1,), (1,)), ((), ())), preferred_element_type=f32)
    current = lax.dynamic_slice_in_dim(base, tp_index * feat_block, feat_block, 1)
    input_term = lax.dynamic_update_slice_in_dim(base, current + side, tp_index * feat_block, 1)
    grad_normed = lax.psum_scatter(
        input_term.astype(jnp.bfloat16), "tp", scatter_dimension=1, tiled=True
    ).astype(jnp.float32)
    scaled = grad_normed * norm_gain[None, :]
    inner_part = jnp.sum(scaled * mixed_in, axis=1)
    inner = lax.psum(inner_part, "tp") / (feat_block * n_tp)
    grad_in = inv_rms[:, None] * scaled - mixed_in * (inv_rms**3 * inner)[:, None]
    grad_streams = (
        carry[None, :, None] * error[:, None, :] + hc_read[None, :, None] * grad_in[:, None, :]
    )
    return (grad_streams.astype(bf16)[None], loss_value)


BLOCK = 256


def dot_rows(left, right):
    return lax.dot_general(left, right, (((1,), (1,)), ((), ())), preferred_element_type=jnp.float32)


def dot_cols(left, right):
    return lax.dot_general(left, right, (((0,), (0,)), ((), ())), preferred_element_type=jnp.float32)


def block_probs(query, keys, start):
    rows, width = query.shape[0], keys.shape[0]
    expo = jnp.exp(dot_rows(query, keys) * HD ** (-0.5))
    row = start + lax.broadcasted_iota(jnp.int32, (rows, width), 0)
    col = lax.broadcasted_iota(jnp.int32, (rows, width), 1)
    expo = jnp.where(col <= row, expo, 0.0)
    return expo / jnp.sum(expo, axis=1, keepdims=True)


def attend_kernel(start_ref, query_ref, keys_ref, vals_ref, out_ref):
    for row in range(0, query_ref.shape[0], BLOCK):
        rows = slice(row, row + BLOCK)
        probs = block_probs(query_ref[rows, :], keys_ref[...], start_ref[0] + row)
        out_ref[rows, :] = jnp.dot(
            probs.astype(jnp.bfloat16), vals_ref[...], preferred_element_type=jnp.float32
        ).astype(jnp.bfloat16)


def attend(start, query, keys, vals):
    length, width = query.shape
    heads = pl.BlockSpec((length, HD), lambda h: (0, h))
    whole = pl.BlockSpec(keys.shape, lambda h: (0, 0))
    return pl.pallas_call(
        attend_kernel,
        grid=(width // HD,),
        in_specs=[pl.BlockSpec(memory_space=pltpu.SMEM), heads, whole, whole],
        out_specs=heads,
        out_shape=jax.ShapeDtypeStruct((length, width), jnp.bfloat16),
        compiler_params=pltpu.CompilerParams(vmem_limit_bytes=32 * 2**20),
        cost_estimate=pl.CostEstimate(
            flops=length * length * width * 8, bytes_accessed=length * width * 6, transcendentals=0
        ),
        name="attend",
    )(start, query, keys, vals)


def attend_grad_kernel(
    start_ref, query_ref, keys_ref, vals_ref, att_ref, grad_ref, gq_ref, gk_ref, gv_ref
):
    @pl.when(pl.program_id(0) == 0)
    def _():
        gk_ref[...] = jnp.zeros_like(gk_ref)
        gv_ref[...] = jnp.zeros_like(gv_ref)

    scale = HD ** (-0.5)
    keys = keys_ref[...]
    for row in range(0, query_ref.shape[0], BLOCK):
        rows = slice(row, row + BLOCK)
        query = query_ref[rows, :]
        grad = grad_ref[rows, :]
        probs = block_probs(query, keys, start_ref[0] + row)
        delta = jnp.sum(
            grad.astype(jnp.float32) * att_ref[rows, :].astype(jnp.float32), axis=1, keepdims=True
        )
        grad_scores = (probs * (dot_rows(grad, vals_ref[...]) - delta)).astype(jnp.bfloat16)
        gq_ref[rows, :] = (
            jnp.dot(grad_scores, keys, preferred_element_type=jnp.float32) * scale
        ).astype(jnp.bfloat16)
        gk_ref[...] += dot_cols(grad_scores, query) * scale
        gv_ref[...] += dot_cols(probs.astype(jnp.bfloat16), grad)


def attend_grad(start, query, keys, vals, att, grad):
    length, width = query.shape
    heads = pl.BlockSpec((length, HD), lambda h: (0, h))
    whole = pl.BlockSpec(keys.shape, lambda h: (0, 0))
    kv_shape = jax.ShapeDtypeStruct(keys.shape, jnp.float32)
    return pl.pallas_call(
        attend_grad_kernel,
        grid=(width // HD,),
        in_specs=[pl.BlockSpec(memory_space=pltpu.SMEM), heads, whole, whole, heads, heads],
        out_specs=[heads, whole, whole],
        out_shape=[jax.ShapeDtypeStruct((length, width), jnp.bfloat16), kv_shape, kv_shape],
        compiler_params=pltpu.CompilerParams(vmem_limit_bytes=32 * 2**20),
        cost_estimate=pl.CostEstimate(
            flops=length * length * width * 16, bytes_accessed=length * width * 8, transcendentals=0
        ),
        name="attend_grad",
    )(start, query, keys, vals, att, grad)


def per_device_heads(
    teacher_rows,
    teacher_gain,
    proj,
    streams,
    hc_read,
    hc_mix,
    hc_write,
    norm_gain,
    w_query,
    w_kv,
    w_out,
):
    f32 = jnp.float32
    bf16 = jnp.bfloat16
    n_seq = lax.axis_size("seq")
    n_tp = lax.axis_size("tp")
    s = lax.axis_index("seq")
    t = lax.axis_index("tp")
    x, c = t // 2, t % 2
    length = teacher_rows.shape[1]
    whole_len = length * n_seq
    feat = streams.shape[3]
    features = feat * n_tp
    every = [(a, b, d) for a in range(2) for b in range(2) for d in range(2)]
    near_pairs = [(4 * a + 2 * b + d, 4 * b + 2 * a + d) for a, b, d in every]
    far_pairs = [(4 * a + 2 * b + d, 4 * b + 2 * (1 - a) + d) for a, b, d in every]
    back_pairs = [(there, here) for here, there in far_pairs]

    def swap(array):
        return lax.ppermute(array, "seq", [(0, 1), (1, 0)])

    def core_swap(array):
        return lax.ppermute(array, "tp", [(i, i ^ 1) for i in range(4)])

    def chip_swap(array):
        return lax.ppermute(array, "tp", [(i, i ^ 2) for i in range(4)])

    def move(array, pairs):
        return lax.ppermute(array, ("seq", "tp"), pairs)

    def half(array, index, axis):
        size = array.shape[axis] // 2
        return lax.dynamic_slice_in_dim(array, index * size, size, axis)

    def by(index, own, other, axis):
        low = jnp.where(index == 0, own, other)
        high = jnp.where(index == 0, other, own)
        return jnp.concatenate([low, high], axis=axis)

    def across_cores(array):
        return by(c, array, core_swap(array), 1)

    def reduce_cores(term):
        got = core_swap(half(term, 1 - c, 1).astype(bf16))
        return half(term, c, 1) + got.astype(f32)

    def after(array, *others):
        return lax.optimization_barrier((array, *others))[0]

    hidden = streams[0].astype(f32)
    mixed_in = jnp.sum(hidden * hc_read[None, :, None], axis=1)
    teacher_f = teacher_rows[0].astype(f32)
    sums = jnp.stack([jnp.sum(mixed_in * mixed_in, axis=1), jnp.sum(teacher_f * teacher_f, axis=1)])
    sums = lax.psum(sums, "tp")
    inv_rms = lax.rsqrt(sums[0] / features + epsilon)
    inv_t = lax.rsqrt(sums[1] / (teacher_f.shape[1] * n_tp) + epsilon)
    normed_s = (mixed_in * inv_rms[:, None] * norm_gain[None, :]).astype(bf16)
    in_far = move(normed_s, far_pairs)
    in_near = move(normed_s, near_pairs)

    kv_part = jnp.dot(normed_s, w_kv, preferred_element_type=f32).astype(bf16)
    kv_sums = [
        lax.psum_scatter(part, "tp", scatter_dimension=1, tiled=True)
        for part in (half(kv_part, 0, 1), half(kv_part, 1, 1))
    ]
    kv_sum = jnp.stack(kv_sums, axis=1)
    kv = by(s, half(kv_sum, s, 2), swap(half(kv_sum, 1 - s, 2)), 0)
    keys, vals = kv[:, 0], kv[:, 1]

    normed_t = (teacher_f * inv_t[:, None] * teacher_gain[None, :]).astype(bf16)
    normed_t = after(normed_t, in_far, in_near)
    teacher_got = swap(normed_t)

    def target_terms(position):
        rows = jnp.where(s == position, normed_t, teacher_got)
        return lax.optimization_barrier(jnp.dot(rows, proj, preferred_element_type=f32))

    query_here, query_there = half(w_query, s, 1), half(w_query, 1 - s, 1)
    out_here, out_there = half(w_out, s, 0), half(w_out, 1 - s, 0)

    def queries(part):
        rows = across_cores(part)
        got = swap(jnp.dot(rows, query_there, preferred_element_type=f32).astype(bf16))
        own = jnp.dot(rows, query_here, preferred_element_type=f32)
        return (own + got.astype(f32)).astype(bf16)

    def output_terms(attended, target):
        got = swap(attended)
        term = jnp.dot(attended, out_here, preferred_element_type=f32)
        term = term + jnp.dot(got, out_there, preferred_element_type=f32)
        return reduce_cores(write * term - target)

    def attended_grads(grad):
        rows = across_cores(grad)
        got = swap(dot_rows(rows, out_there).astype(bf16))
        return (dot_rows(rows, out_here) + got.astype(f32)).astype(bf16)

    def input_terms(grad_query):
        got = swap(grad_query)
        term = dot_rows(grad_query, query_here) + dot_rows(got, query_there)
        return reduce_cores(term).astype(bf16)

    carry = jnp.sum(hc_mix, axis=0)
    write = jnp.sum(hc_write)
    near_start = (x * length).astype(jnp.int32).reshape(1)
    far_start = ((1 - x) * length).astype(jnp.int32).reshape(1)

    query_far = queries(in_far)
    query_near = queries(in_near)
    target_far = target_terms(1 - x)
    target_near = target_terms(x)
    attended_far = attend(far_start, query_far, keys, vals)
    attended_near = attend(near_start, query_near, keys, vals)
    carried = jnp.sum(hidden * carry[None, :, None], axis=1).astype(bf16)
    carried = move(after(carried, query_near), near_pairs).astype(f32)
    term_far = output_terms(attended_far, target_far)
    term_got = chip_swap(term_far.astype(bf16))
    term_near = output_terms(attended_near, target_near)
    error = carried + term_near + term_got.astype(f32)
    loss_part = jnp.sum(error * error)

    grad_out = (write * error).astype(bf16)
    grad_out_far = chip_swap(grad_out)
    grad_near = attended_grads(grad_out)
    gq_near, gk_near, gv_near = attend_grad(
        near_start, query_near, keys, vals, attended_near, grad_near
    )
    grad_far = attended_grads(grad_out_far)
    base_near = move(input_terms(gq_near), near_pairs)
    gq_far, gk_far, gv_far = attend_grad(far_start, query_far, keys, vals, attended_far, grad_far)
    base_far = move(input_terms(gq_far), back_pairs)
    error_back = move(after(error.astype(bf16), gq_near), near_pairs).astype(f32)

    grad_kv = jnp.stack([gk_near + gk_far, gv_near + gv_far], axis=1).astype(bf16)
    grad_kv_own = by(s, half(grad_kv, s, 0), swap(half(grad_kv, 1 - s, 0)), 2)
    grad_kv_all = lax.all_gather(grad_kv_own, "tp", axis=2, tiled=True).reshape(length, -1)
    side = dot_rows(grad_kv_all, w_kv)

    base = base_near.astype(f32) + base_far.astype(f32)
    scaled = (base + side) * norm_gain[None, :]
    inner_part = jnp.sum(scaled * mixed_in, axis=1)
    shared = jnp.concatenate([inner_part, jnp.full((HD,), loss_part, f32)])
    shared = lax.all_gather(shared, ("role", "seq", "tp"), axis=0)
    n_role = lax.axis_size("role")
    loss_value = jnp.sum(shared[:, length]) / (n_role * whole_len * features)
    place = (lax.axis_index("role") * n_seq + s) * n_tp
    shared = lax.dynamic_slice_in_dim(shared, place, n_tp, 0)
    inner = jnp.sum(shared[:, :length], axis=0) / features
    grad_in = inv_rms[:, None] * scaled - mixed_in * (inv_rms**3 * inner)[:, None]
    grad_streams = (
        carry[None, :, None] * error_back[:, None, :] + hc_read[None, :, None] * grad_in[:, None, :]
    )
    return (grad_streams.astype(bf16)[None], loss_value)


def solution(mesh):
    placed = (
        P("role", "seq", "tp"),
        P("tp"),
        P("tp", "seq"),
        P("role", "seq", None, "tp"),
        P(),
        P(),
        P(),
        P("tp"),
        P("seq", "tp"),
        P("tp", None),
        P("tp", "seq"),
    )
    seq, tp = mesh.shape["seq"], mesh.shape["tp"]
    by_heads = seq == 2 and tp == 4
    return jax.shard_map(
        per_device_heads if by_heads else per_device_rows,
        mesh=mesh,
        in_specs=placed,
        out_specs=(P("role", "seq", None, "tp"), P()),
        check_vma=False,
    )
```

```python
import jax
import jax.numpy as jnp
from jax import lax
from jax.experimental import pallas as pl
from jax.experimental.pallas import tpu as pltpu
from jax.sharding import PartitionSpec as P

HEADS = 32
KVH = 8
HD = 128


epsilon = 1e-05


def per_device_rows(
    teacher_rows,
    teacher_gain,
    proj,
    streams,
    hc_read,
    hc_mix,
    hc_write,
    norm_gain,
    w_query,
    w_kv,
    w_out,
):
    f32 = jnp.float32
    bf16 = jnp.bfloat16
    n_tp = lax.axis_size("tp")
    tp_index = lax.axis_index("tp")
    seq_index = lax.axis_index("seq")
    teacher = teacher_rows[0].astype(f32)
    hidden = streams[0].astype(f32)
    mixed_in = jnp.sum(hidden * hc_read[None, :, None], axis=1)
    feat_block = mixed_in.shape[1]
    teacher_sq, student_sq = lax.psum(
        (jnp.sum(teacher * teacher, axis=1), jnp.sum(mixed_in * mixed_in, axis=1)), "tp"
    )
    inv_t = lax.rsqrt(teacher_sq / (teacher.shape[1] * n_tp) + epsilon)
    normed_t = (teacher * inv_t[:, None] * teacher_gain[None, :]).astype(bf16)
    local_len = normed_t.shape[0]
    proj_full = lax.all_gather(proj, "seq", axis=1, tiled=True)
    target_term = jnp.dot(normed_t, proj_full, preferred_element_type=f32)
    target = lax.psum_scatter(
        target_term.astype(jnp.bfloat16), "tp", scatter_dimension=1, tiled=True
    ).astype(jnp.float32)
    inv_rms = lax.rsqrt(student_sq / (feat_block * n_tp) + epsilon)
    normed_s = (mixed_in * inv_rms[:, None] * norm_gain[None, :]).astype(bf16)
    heads_dev = w_query.shape[1] // HD
    group = HEADS // KVH
    kv_dev = max(1, heads_dev // group)
    per_kv = heads_dev // kv_dev
    ratio = max(1, group // heads_dev)
    first = tp_index * heads_dev // group
    query_full = lax.all_gather(w_query, "seq", axis=0, tiled=True)
    kv_part = jnp.dot(normed_s, w_kv, preferred_element_type=f32)
    kv_all = lax.psum(kv_part.astype(jnp.bfloat16), "tp").astype(jnp.float32).astype(bf16)
    keys_own = lax.dynamic_slice_in_dim(kv_all, first * HD, kv_dev * HD, 1)
    vals_own = lax.dynamic_slice_in_dim(kv_all, (KVH + first) * HD, kv_dev * HD, 1)
    rows_full = lax.all_gather(normed_s, "tp", axis=1, tiled=True)
    query = jnp.dot(rows_full, query_full, preferred_element_type=f32).astype(bf16)
    keys_all, vals_all = (
        lax.all_gather(keys_own, "seq", axis=0, tiled=True),
        lax.all_gather(vals_own, "seq", axis=0, tiled=True),
    )
    whole_len = keys_all.shape[0]
    scale = HD ** (-0.5)
    query4 = query.reshape(local_len, kv_dev, per_kv, HD)
    keys3 = keys_all.reshape(whole_len, kv_dev, HD)
    vals3 = vals_all.reshape(whole_len, kv_dev, HD)
    scores = jnp.einsum("qgjd,kgd->gjqk", query4, keys3, preferred_element_type=f32) * scale
    query_pos = seq_index * local_len + lax.iota(jnp.int32, local_len)
    key_pos = lax.iota(jnp.int32, whole_len)
    allowed = key_pos[None, :] <= query_pos[:, None]
    scores = jnp.where(allowed, scores, -1e30)
    expo = jnp.exp(scores)
    probs = expo / jnp.sum(expo, axis=-1, keepdims=True)
    probs_low = probs.astype(bf16)
    attended = jnp.einsum("gjqk,kgd->qgjd", probs_low, vals3, preferred_element_type=f32).astype(
        bf16
    )
    attended = attended.reshape(local_len, heads_dev * HD)
    out_full = lax.all_gather(w_out, "seq", axis=1, tiled=True)
    out_term = jnp.dot(attended, out_full, preferred_element_type=f32)
    layer_out = lax.psum_scatter(
        out_term.astype(jnp.bfloat16), "tp", scatter_dimension=1, tiled=True
    ).astype(jnp.float32)
    carry = jnp.sum(hc_mix, axis=0)
    write = jnp.sum(hc_write)
    student = jnp.sum(hidden * carry[None, :, None], axis=1) + write * layer_out
    error = student - target
    loss_total = lax.psum(jnp.sum(error * error), ("role", "seq", "tp"))
    loss_value = loss_total / (lax.axis_size("role") * whole_len * feat_block * n_tp)
    grad_out = (write * error).astype(bf16)
    grad_full = lax.all_gather(grad_out, "tp", axis=1, tiled=True)
    grad_att = lax.dot_general(
        grad_full, out_full, (((1,), (1,)), ((), ())), preferred_element_type=f32
    ).astype(bf16)
    grad4 = grad_att.reshape(local_len, kv_dev, per_kv, HD)
    att4 = attended.reshape(local_len, kv_dev, per_kv, HD)
    grad_probs = jnp.einsum("qgjd,kgd->gjqk", grad4, vals3, preferred_element_type=f32)
    delta = jnp.einsum("qgjd,qgjd->gjq", grad4, att4, preferred_element_type=f32)
    grad_scores = (probs * (grad_probs - delta[..., None])).astype(bf16)
    grad_query = (
        jnp.einsum("gjqk,kgd->qgjd", grad_scores, keys3, preferred_element_type=f32) * scale
    ).astype(bf16)
    grad_query = grad_query.reshape(local_len, heads_dev * HD)
    grad_keys = (
        jnp.einsum("gjqk,qgjd->kgd", grad_scores, query4, preferred_element_type=f32) * scale
    )
    grad_vals = jnp.einsum("gjqk,qgjd->kgd", probs_low, grad4, preferred_element_type=f32)
    key_sum, val_sum = (
        lax.psum_scatter(
            grad_keys.reshape(whole_len, kv_dev * HD).astype(jnp.bfloat16),
            "seq",
            scatter_dimension=0,
            tiled=True,
        ).astype(jnp.float32),
        lax.psum_scatter(
            grad_vals.reshape(whole_len, kv_dev * HD).astype(jnp.bfloat16),
            "seq",
            scatter_dimension=0,
            tiled=True,
        ).astype(jnp.float32),
    )
    key_parts, val_parts = (
        lax.all_gather(key_sum.astype(bf16), "tp", axis=1, tiled=True),
        lax.all_gather(val_sum.astype(bf16), "tp", axis=1, tiled=True),
    )
    key_grad = jnp.sum(
        key_parts.astype(f32).reshape(local_len, n_tp // ratio, ratio, kv_dev * HD), axis=2
    )
    val_grad = jnp.sum(
        val_parts.astype(f32).reshape(local_len, n_tp // ratio, ratio, kv_dev * HD), axis=2
    )
    grad_kv = jnp.concatenate(
        [key_grad.reshape(local_len, KVH * HD), val_grad.reshape(local_len, KVH * HD)], axis=1
    ).astype(bf16)
    base = lax.dot_general(
        grad_query, query_full, (((1,), (1,)), ((), ())), preferred_element_type=f32
    )
    side = lax.dot_general(grad_kv, w_kv, (((1,), (1,)), ((), ())), preferred_element_type=f32)
    current = lax.dynamic_slice_in_dim(base, tp_index * feat_block, feat_block, 1)
    input_term = lax.dynamic_update_slice_in_dim(base, current + side, tp_index * feat_block, 1)
    grad_normed = lax.psum_scatter(
        input_term.astype(jnp.bfloat16), "tp", scatter_dimension=1, tiled=True
    ).astype(jnp.float32)
    scaled = grad_normed * norm_gain[None, :]
    inner_part = jnp.sum(scaled * mixed_in, axis=1)
    inner = lax.psum(inner_part, "tp") / (feat_block * n_tp)
    grad_in = inv_rms[:, None] * scaled - mixed_in * (inv_rms**3 * inner)[:, None]
    grad_streams = (
        carry[None, :, None] * error[:, None, :] + hc_read[None, :, None] * grad_in[:, None, :]
    )
    return (grad_streams.astype(bf16)[None], loss_value)


BLOCK = 256


def dot_rows(left, right):
    return lax.dot_general(left, right, (((1,), (1,)), ((), ())), preferred_element_type=jnp.float32)


def dot_cols(left, right):
    return lax.dot_general(left, right, (((0,), (0,)), ((), ())), preferred_element_type=jnp.float32)


def block_probs(query, keys, start):
    rows, width = query.shape[0], keys.shape[0]
    expo = jnp.exp(dot_rows(query, keys) * HD ** (-0.5))
    row = start + lax.broadcasted_iota(jnp.int32, (rows, width), 0)
    col = lax.broadcasted_iota(jnp.int32, (rows, width), 1)
    expo = jnp.where(col <= row, expo, 0.0)
    return expo / jnp.sum(expo, axis=1, keepdims=True)


def attend_kernel(start_ref, query_ref, keys_ref, vals_ref, out_ref):
    for row in range(0, query_ref.shape[0], BLOCK):
        rows = slice(row, row + BLOCK)
        probs = block_probs(query_ref[rows, :], keys_ref[...], start_ref[0] + row)
        out_ref[rows, :] = jnp.dot(
            probs.astype(jnp.bfloat16), vals_ref[...], preferred_element_type=jnp.float32
        ).astype(jnp.bfloat16)


def attend(start, query, keys, vals):
    length, width = query.shape
    heads = pl.BlockSpec((length, HD), lambda h: (0, h))
    whole = pl.BlockSpec(keys.shape, lambda h: (0, 0))
    return pl.pallas_call(
        attend_kernel,
        grid=(width // HD,),
        in_specs=[pl.BlockSpec(memory_space=pltpu.SMEM), heads, whole, whole],
        out_specs=heads,
        out_shape=jax.ShapeDtypeStruct((length, width), jnp.bfloat16),
        compiler_params=pltpu.CompilerParams(vmem_limit_bytes=32 * 2**20),
        cost_estimate=pl.CostEstimate(
            flops=length * length * width * 8, bytes_accessed=length * width * 6, transcendentals=0
        ),
        name="attend",
    )(start, query, keys, vals)


def attend_grad_kernel(
    start_ref, query_ref, keys_ref, vals_ref, att_ref, grad_ref, gq_ref, gk_ref, gv_ref
):
    @pl.when(pl.program_id(0) == 0)
    def _():
        gk_ref[...] = jnp.zeros_like(gk_ref)
        gv_ref[...] = jnp.zeros_like(gv_ref)

    scale = HD ** (-0.5)
    keys = keys_ref[...]
    for row in range(0, query_ref.shape[0], BLOCK):
        rows = slice(row, row + BLOCK)
        query = query_ref[rows, :]
        grad = grad_ref[rows, :]
        probs = block_probs(query, keys, start_ref[0] + row)
        delta = jnp.sum(
            grad.astype(jnp.float32) * att_ref[rows, :].astype(jnp.float32), axis=1, keepdims=True
        )
        grad_scores = (probs * (dot_rows(grad, vals_ref[...]) - delta)).astype(jnp.bfloat16)
        gq_ref[rows, :] = (
            jnp.dot(grad_scores, keys, preferred_element_type=jnp.float32) * scale
        ).astype(jnp.bfloat16)
        gk_ref[...] += dot_cols(grad_scores, query) * scale
        gv_ref[...] += dot_cols(probs.astype(jnp.bfloat16), grad)


def attend_grad(start, query, keys, vals, att, grad):
    length, width = query.shape
    heads = pl.BlockSpec((length, HD), lambda h: (0, h))
    whole = pl.BlockSpec(keys.shape, lambda h: (0, 0))
    kv_shape = jax.ShapeDtypeStruct(keys.shape, jnp.float32)
    return pl.pallas_call(
        attend_grad_kernel,
        grid=(width // HD,),
        in_specs=[pl.BlockSpec(memory_space=pltpu.SMEM), heads, whole, whole, heads, heads],
        out_specs=[heads, whole, whole],
        out_shape=[jax.ShapeDtypeStruct((length, width), jnp.bfloat16), kv_shape, kv_shape],
        compiler_params=pltpu.CompilerParams(vmem_limit_bytes=32 * 2**20),
        cost_estimate=pl.CostEstimate(
            flops=length * length * width * 16, bytes_accessed=length * width * 8, transcendentals=0
        ),
        name="attend_grad",
    )(start, query, keys, vals, att, grad)


def per_device_heads(
    teacher_rows,
    teacher_gain,
    proj,
    streams,
    hc_read,
    hc_mix,
    hc_write,
    norm_gain,
    w_query,
    w_kv,
    w_out,
):
    f32 = jnp.float32
    bf16 = jnp.bfloat16
    n_seq = lax.axis_size("seq")
    n_tp = lax.axis_size("tp")
    s = lax.axis_index("seq")
    t = lax.axis_index("tp")
    x, c = t // 2, t % 2
    length = teacher_rows.shape[1]
    whole_len = length * n_seq
    feat = streams.shape[3]
    features = feat * n_tp
    every = [(a, b, d) for a in range(2) for b in range(2) for d in range(2)]
    near_pairs = [(4 * a + 2 * b + d, 4 * b + 2 * a + d) for a, b, d in every]
    far_pairs = [(4 * a + 2 * b + d, 4 * b + 2 * (1 - a) + d) for a, b, d in every]
    back_pairs = [(there, here) for here, there in far_pairs]

    def swap(array):
        return lax.ppermute(array, "seq", [(0, 1), (1, 0)])

    def core_swap(array):
        return lax.ppermute(array, "tp", [(i, i ^ 1) for i in range(4)])

    def chip_swap(array):
        return lax.ppermute(array, "tp", [(i, i ^ 2) for i in range(4)])

    def move(array, pairs):
        return lax.ppermute(array, ("seq", "tp"), pairs)

    def half(array, index, axis):
        size = array.shape[axis] // 2
        return lax.dynamic_slice_in_dim(array, index * size, size, axis)

    def by(index, own, other, axis):
        low = jnp.where(index == 0, own, other)
        high = jnp.where(index == 0, other, own)
        return jnp.concatenate([low, high], axis=axis)

    def across_cores(array):
        return by(c, array, core_swap(array), 1)

    def reduce_cores(term):
        got = core_swap(half(term, 1 - c, 1).astype(bf16))
        return half(term, c, 1) + got.astype(f32)

    def after(array, *others):
        return lax.optimization_barrier((array, *others))[0]

    teacher_got = swap(teacher_rows[0])
    hidden = streams[0].astype(f32)
    mixed_in = jnp.sum(hidden * hc_read[None, :, None], axis=1)
    teacher_f = teacher_rows[0].astype(f32)
    sums = jnp.stack([jnp.sum(mixed_in * mixed_in, axis=1), jnp.sum(teacher_f * teacher_f, axis=1)])
    sums = lax.psum(sums, "tp")
    inv_rms = lax.rsqrt(sums[0] / features + epsilon)
    inv_t = lax.rsqrt(sums[1] / (teacher_f.shape[1] * n_tp) + epsilon)
    normed_s = (mixed_in * inv_rms[:, None] * norm_gain[None, :]).astype(bf16)
    in_far = move(normed_s, far_pairs)
    in_near = move(normed_s, near_pairs)

    kv_part = jnp.dot(after(normed_s, teacher_got), w_kv, preferred_element_type=f32).astype(bf16)
    kv_sums = [
        lax.psum_scatter(part, "tp", scatter_dimension=1, tiled=True)
        for part in (half(kv_part, 0, 1), half(kv_part, 1, 1))
    ]
    kv_sum = jnp.stack(kv_sums, axis=1)
    kv = by(s, half(kv_sum, s, 2), swap(half(kv_sum, 1 - s, 2)), 0)
    keys, vals = kv[:, 0], kv[:, 1]

    inv_t_got = swap(inv_t)

    def target_terms(position):
        rows = jnp.where(s == position, teacher_rows[0], teacher_got).astype(f32)
        inv = jnp.where(s == position, inv_t, inv_t_got)
        rows = (rows * inv[:, None] * teacher_gain[None, :]).astype(bf16)
        return lax.optimization_barrier(jnp.dot(rows, proj, preferred_element_type=f32))

    query_here, query_there = half(w_query, s, 1), half(w_query, 1 - s, 1)
    out_here, out_there = half(w_out, s, 0), half(w_out, 1 - s, 0)

    def queries(part):
        rows = across_cores(part)
        got = swap(jnp.dot(rows, query_there, preferred_element_type=f32).astype(bf16))
        own = jnp.dot(rows, query_here, preferred_element_type=f32)
        return (own + got.astype(f32)).astype(bf16)

    def output_terms(attended, target):
        got = swap(attended)
        term = jnp.dot(attended, out_here, preferred_element_type=f32)
        term = term + jnp.dot(got, out_there, preferred_element_type=f32)
        return reduce_cores(write * term - target)

    def attended_grads(grad):
        rows = across_cores(grad)
        far_term = dot_rows(rows, out_there).astype(bf16)
        got = swap(far_term)
        return (dot_rows(rows, out_here) + got.astype(f32)).astype(bf16), far_term

    def input_terms(grad_query):
        got = swap(grad_query)
        term = dot_rows(grad_query, query_here) + dot_rows(got, query_there)
        return reduce_cores(term).astype(bf16)

    carry = jnp.sum(hc_mix, axis=0)
    write = jnp.sum(hc_write)
    near_start = (x * length).astype(jnp.int32).reshape(1)
    far_start = ((1 - x) * length).astype(jnp.int32).reshape(1)

    query_far = queries(in_far)
    query_near = queries(in_near)
    target_far = target_terms(1 - x)
    target_near = target_terms(x)
    query_far = after(query_far, target_far)
    query_near = after(query_near, target_near)
    attended_far = attend(far_start, query_far, keys, vals)
    attended_near = attend(near_start, query_near, keys, vals)
    carried = jnp.sum(hidden * carry[None, :, None], axis=1).astype(bf16)
    carried = move(after(carried, query_near), near_pairs).astype(f32)
    term_far = output_terms(attended_far, target_far)
    term_got = chip_swap(term_far.astype(bf16))
    term_near = output_terms(attended_near, target_near)
    error = carried + term_near + term_got.astype(f32)
    loss_part = jnp.sum(error * error, axis=0, keepdims=True)
    loss_part = jnp.sum(loss_part.reshape(-1, HD), axis=0, keepdims=True)
    n_role = lax.axis_size("role")
    for axis, size in (("tp", n_tp), ("seq", n_seq), ("role", n_role)):
        step = 1
        while step < size:
            pairs = [(i, i ^ step) for i in range(size)]
            loss_part = loss_part + lax.ppermute(loss_part, axis, pairs)
            step *= 2
    loss_value = jnp.sum(loss_part) / (n_role * whole_len * features)

    grad_out = (write * error).astype(bf16)
    grad_out_far = chip_swap(grad_out)
    grad_near, near_term = attended_grads(grad_out)
    gq_near, gk_near, gv_near = attend_grad(
        near_start, query_near, keys, vals, attended_near, grad_near
    )
    grad_far, _ = attended_grads(after(grad_out_far, near_term))
    base_near = move(input_terms(gq_near), near_pairs)
    gq_far, gk_far, gv_far = attend_grad(far_start, query_far, keys, vals, attended_far, grad_far)
    base_far = move(input_terms(gq_far), back_pairs)
    error_back = move(after(error.astype(bf16), near_term), near_pairs).astype(f32)

    grad_kv = jnp.stack([gk_near + gk_far, gv_near + gv_far], axis=1).astype(bf16)
    grad_kv_own = by(s, half(grad_kv, s, 0), swap(half(grad_kv, 1 - s, 0)), 2)
    grad_kv_all = lax.all_gather(grad_kv_own, "tp", axis=2, tiled=True).reshape(length, -1)
    side = dot_rows(grad_kv_all, w_kv)

    base = base_near.astype(f32) + base_far.astype(f32)
    scaled = (base + side) * norm_gain[None, :]
    inner_part = jnp.sum(scaled * mixed_in, axis=1)
    inner = lax.psum(inner_part, "tp") / features
    grad_in = inv_rms[:, None] * scaled - mixed_in * (inv_rms**3 * inner)[:, None]
    grad_streams = (
        carry[None, :, None] * error_back[:, None, :] + hc_read[None, :, None] * grad_in[:, None, :]
    )
    return (grad_streams.astype(bf16)[None], loss_value)


def solution(mesh):
    placed = (
        P("role", "seq", "tp"),
        P("tp"),
        P("tp", "seq"),
        P("role", "seq", None, "tp"),
        P(),
        P(),
        P(),
        P("tp"),
        P("seq", "tp"),
        P("tp", None),
        P("tp", "seq"),
    )
    seq, tp = mesh.shape["seq"], mesh.shape["tp"]
    by_heads = seq == 2 and tp == 4 and mesh.shape["role"] in (1, 2, 4, 8)
    return jax.shard_map(
        per_device_heads if by_heads else per_device_rows,
        mesh=mesh,
        in_specs=placed,
        out_specs=(P("role", "seq", None, "tp"), P()),
        check_vma=False,
    )
```

```python
import jax
import jax.numpy as jnp
from jax import lax
from jax.experimental import pallas as pl
from jax.experimental.pallas import tpu as pltpu
from jax.sharding import PartitionSpec as P

HEADS = 32
KVH = 8
HD = 128


epsilon = 1e-05


def per_device_rows(
    teacher_rows,
    teacher_gain,
    proj,
    streams,
    hc_read,
    hc_mix,
    hc_write,
    norm_gain,
    w_query,
    w_kv,
    w_out,
):
    f32 = jnp.float32
    bf16 = jnp.bfloat16
    n_tp = lax.axis_size("tp")
    tp_index = lax.axis_index("tp")
    seq_index = lax.axis_index("seq")
    teacher = teacher_rows[0].astype(f32)
    hidden = streams[0].astype(f32)
    mixed_in = jnp.sum(hidden * hc_read[None, :, None], axis=1)
    feat_block = mixed_in.shape[1]
    teacher_sq, student_sq = lax.psum(
        (jnp.sum(teacher * teacher, axis=1), jnp.sum(mixed_in * mixed_in, axis=1)), "tp"
    )
    inv_t = lax.rsqrt(teacher_sq / (teacher.shape[1] * n_tp) + epsilon)
    normed_t = (teacher * inv_t[:, None] * teacher_gain[None, :]).astype(bf16)
    local_len = normed_t.shape[0]
    proj_full = lax.all_gather(proj, "seq", axis=1, tiled=True)
    target_term = jnp.dot(normed_t, proj_full, preferred_element_type=f32)
    target = lax.psum_scatter(
        target_term.astype(jnp.bfloat16), "tp", scatter_dimension=1, tiled=True
    ).astype(jnp.float32)
    inv_rms = lax.rsqrt(student_sq / (feat_block * n_tp) + epsilon)
    normed_s = (mixed_in * inv_rms[:, None] * norm_gain[None, :]).astype(bf16)
    heads_dev = w_query.shape[1] // HD
    group = HEADS // KVH
    kv_dev = max(1, heads_dev // group)
    per_kv = heads_dev // kv_dev
    ratio = max(1, group // heads_dev)
    first = tp_index * heads_dev // group
    query_full = lax.all_gather(w_query, "seq", axis=0, tiled=True)
    kv_part = jnp.dot(normed_s, w_kv, preferred_element_type=f32)
    kv_all = lax.psum(kv_part.astype(jnp.bfloat16), "tp").astype(jnp.float32).astype(bf16)
    keys_own = lax.dynamic_slice_in_dim(kv_all, first * HD, kv_dev * HD, 1)
    vals_own = lax.dynamic_slice_in_dim(kv_all, (KVH + first) * HD, kv_dev * HD, 1)
    rows_full = lax.all_gather(normed_s, "tp", axis=1, tiled=True)
    query = jnp.dot(rows_full, query_full, preferred_element_type=f32).astype(bf16)
    keys_all, vals_all = (
        lax.all_gather(keys_own, "seq", axis=0, tiled=True),
        lax.all_gather(vals_own, "seq", axis=0, tiled=True),
    )
    whole_len = keys_all.shape[0]
    scale = HD ** (-0.5)
    query4 = query.reshape(local_len, kv_dev, per_kv, HD)
    keys3 = keys_all.reshape(whole_len, kv_dev, HD)
    vals3 = vals_all.reshape(whole_len, kv_dev, HD)
    scores = jnp.einsum("qgjd,kgd->gjqk", query4, keys3, preferred_element_type=f32) * scale
    query_pos = seq_index * local_len + lax.iota(jnp.int32, local_len)
    key_pos = lax.iota(jnp.int32, whole_len)
    allowed = key_pos[None, :] <= query_pos[:, None]
    scores = jnp.where(allowed, scores, -1e30)
    expo = jnp.exp(scores)
    probs = expo / jnp.sum(expo, axis=-1, keepdims=True)
    probs_low = probs.astype(bf16)
    attended = jnp.einsum("gjqk,kgd->qgjd", probs_low, vals3, preferred_element_type=f32).astype(
        bf16
    )
    attended = attended.reshape(local_len, heads_dev * HD)
    out_full = lax.all_gather(w_out, "seq", axis=1, tiled=True)
    out_term = jnp.dot(attended, out_full, preferred_element_type=f32)
    layer_out = lax.psum_scatter(
        out_term.astype(jnp.bfloat16), "tp", scatter_dimension=1, tiled=True
    ).astype(jnp.float32)
    carry = jnp.sum(hc_mix, axis=0)
    write = jnp.sum(hc_write)
    student = jnp.sum(hidden * carry[None, :, None], axis=1) + write * layer_out
    error = student - target
    loss_total = lax.psum(jnp.sum(error * error), ("role", "seq", "tp"))
    loss_value = loss_total / (lax.axis_size("role") * whole_len * feat_block * n_tp)
    grad_out = (write * error).astype(bf16)
    grad_full = lax.all_gather(grad_out, "tp", axis=1, tiled=True)
    grad_att = lax.dot_general(
        grad_full, out_full, (((1,), (1,)), ((), ())), preferred_element_type=f32
    ).astype(bf16)
    grad4 = grad_att.reshape(local_len, kv_dev, per_kv, HD)
    att4 = attended.reshape(local_len, kv_dev, per_kv, HD)
    grad_probs = jnp.einsum("qgjd,kgd->gjqk", grad4, vals3, preferred_element_type=f32)
    delta = jnp.einsum("qgjd,qgjd->gjq", grad4, att4, preferred_element_type=f32)
    grad_scores = (probs * (grad_probs - delta[..., None])).astype(bf16)
    grad_query = (
        jnp.einsum("gjqk,kgd->qgjd", grad_scores, keys3, preferred_element_type=f32) * scale
    ).astype(bf16)
    grad_query = grad_query.reshape(local_len, heads_dev * HD)
    grad_keys = (
        jnp.einsum("gjqk,qgjd->kgd", grad_scores, query4, preferred_element_type=f32) * scale
    )
    grad_vals = jnp.einsum("gjqk,qgjd->kgd", probs_low, grad4, preferred_element_type=f32)
    key_sum, val_sum = (
        lax.psum_scatter(
            grad_keys.reshape(whole_len, kv_dev * HD).astype(jnp.bfloat16),
            "seq",
            scatter_dimension=0,
            tiled=True,
        ).astype(jnp.float32),
        lax.psum_scatter(
            grad_vals.reshape(whole_len, kv_dev * HD).astype(jnp.bfloat16),
            "seq",
            scatter_dimension=0,
            tiled=True,
        ).astype(jnp.float32),
    )
    key_parts, val_parts = (
        lax.all_gather(key_sum.astype(bf16), "tp", axis=1, tiled=True),
        lax.all_gather(val_sum.astype(bf16), "tp", axis=1, tiled=True),
    )
    key_grad = jnp.sum(
        key_parts.astype(f32).reshape(local_len, n_tp // ratio, ratio, kv_dev * HD), axis=2
    )
    val_grad = jnp.sum(
        val_parts.astype(f32).reshape(local_len, n_tp // ratio, ratio, kv_dev * HD), axis=2
    )
    grad_kv = jnp.concatenate(
        [key_grad.reshape(local_len, KVH * HD), val_grad.reshape(local_len, KVH * HD)], axis=1
    ).astype(bf16)
    base = lax.dot_general(
        grad_query, query_full, (((1,), (1,)), ((), ())), preferred_element_type=f32
    )
    side = lax.dot_general(grad_kv, w_kv, (((1,), (1,)), ((), ())), preferred_element_type=f32)
    current = lax.dynamic_slice_in_dim(base, tp_index * feat_block, feat_block, 1)
    input_term = lax.dynamic_update_slice_in_dim(base, current + side, tp_index * feat_block, 1)
    grad_normed = lax.psum_scatter(
        input_term.astype(jnp.bfloat16), "tp", scatter_dimension=1, tiled=True
    ).astype(jnp.float32)
    scaled = grad_normed * norm_gain[None, :]
    inner_part = jnp.sum(scaled * mixed_in, axis=1)
    inner = lax.psum(inner_part, "tp") / (feat_block * n_tp)
    grad_in = inv_rms[:, None] * scaled - mixed_in * (inv_rms**3 * inner)[:, None]
    grad_streams = (
        carry[None, :, None] * error[:, None, :] + hc_read[None, :, None] * grad_in[:, None, :]
    )
    return (grad_streams.astype(bf16)[None], loss_value)


BLOCK = 256


def dot_rows(left, right):
    return lax.dot_general(left, right, (((1,), (1,)), ((), ())), preferred_element_type=jnp.float32)


def dot_cols(left, right):
    return lax.dot_general(left, right, (((0,), (0,)), ((), ())), preferred_element_type=jnp.float32)


def block_probs(query, keys, start):
    rows, width = query.shape[0], keys.shape[0]
    expo = jnp.exp(dot_rows(query, keys) * HD ** (-0.5))
    row = start + lax.broadcasted_iota(jnp.int32, (rows, width), 0)
    col = lax.broadcasted_iota(jnp.int32, (rows, width), 1)
    expo = jnp.where(col <= row, expo, 0.0)
    return expo / jnp.sum(expo, axis=1, keepdims=True)


def attend_kernel(start_ref, query_ref, keys_ref, vals_ref, out_ref):
    for row in range(0, query_ref.shape[0], BLOCK):
        rows = slice(row, row + BLOCK)
        probs = block_probs(query_ref[rows, :], keys_ref[...], start_ref[0] + row)
        out_ref[rows, :] = jnp.dot(
            probs.astype(jnp.bfloat16), vals_ref[...], preferred_element_type=jnp.float32
        ).astype(jnp.bfloat16)


def attend(start, query, keys, vals):
    length, width = query.shape
    heads = pl.BlockSpec((length, HD), lambda h: (0, h))
    whole = pl.BlockSpec(keys.shape, lambda h: (0, 0))
    return pl.pallas_call(
        attend_kernel,
        grid=(width // HD,),
        in_specs=[pl.BlockSpec(memory_space=pltpu.SMEM), heads, whole, whole],
        out_specs=heads,
        out_shape=jax.ShapeDtypeStruct((length, width), jnp.bfloat16),
        compiler_params=pltpu.CompilerParams(vmem_limit_bytes=32 * 2**20),
        cost_estimate=pl.CostEstimate(
            flops=length * length * width * 8, bytes_accessed=length * width * 6, transcendentals=0
        ),
        name="attend",
    )(start, query, keys, vals)


def attend_grad_kernel(
    start_ref, query_ref, keys_ref, vals_ref, att_ref, grad_ref, gq_ref, gk_ref, gv_ref
):
    @pl.when(pl.program_id(0) == 0)
    def _():
        gk_ref[...] = jnp.zeros_like(gk_ref)
        gv_ref[...] = jnp.zeros_like(gv_ref)

    scale = HD ** (-0.5)
    keys = keys_ref[...]
    for row in range(0, query_ref.shape[0], BLOCK):
        rows = slice(row, row + BLOCK)
        query = query_ref[rows, :]
        grad = grad_ref[rows, :]
        probs = block_probs(query, keys, start_ref[0] + row)
        delta = jnp.sum(
            grad.astype(jnp.float32) * att_ref[rows, :].astype(jnp.float32), axis=1, keepdims=True
        )
        grad_scores = (probs * (dot_rows(grad, vals_ref[...]) - delta)).astype(jnp.bfloat16)
        gq_ref[rows, :] = (
            jnp.dot(grad_scores, keys, preferred_element_type=jnp.float32) * scale
        ).astype(jnp.bfloat16)
        gk_ref[...] += dot_cols(grad_scores, query) * scale
        gv_ref[...] += dot_cols(probs.astype(jnp.bfloat16), grad)


def attend_grad(start, query, keys, vals, att, grad):
    length, width = query.shape
    heads = pl.BlockSpec((length, HD), lambda h: (0, h))
    whole = pl.BlockSpec(keys.shape, lambda h: (0, 0))
    kv_shape = jax.ShapeDtypeStruct(keys.shape, jnp.float32)
    return pl.pallas_call(
        attend_grad_kernel,
        grid=(width // HD,),
        in_specs=[pl.BlockSpec(memory_space=pltpu.SMEM), heads, whole, whole, heads, heads],
        out_specs=[heads, whole, whole],
        out_shape=[jax.ShapeDtypeStruct((length, width), jnp.bfloat16), kv_shape, kv_shape],
        compiler_params=pltpu.CompilerParams(vmem_limit_bytes=32 * 2**20),
        cost_estimate=pl.CostEstimate(
            flops=length * length * width * 16, bytes_accessed=length * width * 8, transcendentals=0
        ),
        name="attend_grad",
    )(start, query, keys, vals, att, grad)


def per_device_heads(
    teacher_rows,
    teacher_gain,
    proj,
    streams,
    hc_read,
    hc_mix,
    hc_write,
    norm_gain,
    w_query,
    w_kv,
    w_out,
):
    f32 = jnp.float32
    bf16 = jnp.bfloat16
    n_seq = lax.axis_size("seq")
    n_tp = lax.axis_size("tp")
    s = lax.axis_index("seq")
    t = lax.axis_index("tp")
    x, c = t // 2, t % 2
    length = teacher_rows.shape[1]
    whole_len = length * n_seq
    feat = streams.shape[3]
    features = feat * n_tp
    every = [(a, b, d) for a in range(2) for b in range(2) for d in range(2)]
    near_pairs = [(4 * a + 2 * b + d, 4 * b + 2 * a + d) for a, b, d in every]
    far_pairs = [(4 * a + 2 * b + d, 4 * b + 2 * (1 - a) + d) for a, b, d in every]
    back_pairs = [(there, here) for here, there in far_pairs]

    def swap(array):
        return lax.ppermute(array, "seq", [(0, 1), (1, 0)])

    def core_swap(array):
        return lax.ppermute(array, "tp", [(i, i ^ 1) for i in range(4)])

    def chip_swap(array):
        return lax.ppermute(array, "tp", [(i, i ^ 2) for i in range(4)])

    def move(array, pairs):
        return lax.ppermute(array, ("seq", "tp"), pairs)

    def half(array, index, axis):
        size = array.shape[axis] // 2
        return lax.dynamic_slice_in_dim(array, index * size, size, axis)

    def by(index, own, other, axis):
        low = jnp.where(index == 0, own, other)
        high = jnp.where(index == 0, other, own)
        return jnp.concatenate([low, high], axis=axis)

    def across_cores(array):
        return by(c, array, core_swap(array), 1)

    def reduce_cores(term):
        got = core_swap(half(term, 1 - c, 1).astype(bf16))
        return half(term, c, 1) + got.astype(f32)

    def after(array, *others):
        return lax.optimization_barrier((array, *others))[0]

    teacher_got = swap(teacher_rows[0])
    hidden = streams[0].astype(f32)
    mixed_in = jnp.sum(hidden * hc_read[None, :, None], axis=1)
    teacher_f = teacher_rows[0].astype(f32)
    sums = jnp.stack([jnp.sum(mixed_in * mixed_in, axis=1), jnp.sum(teacher_f * teacher_f, axis=1)])
    sums = lax.psum(sums, "tp")
    inv_rms = lax.rsqrt(sums[0] / features + epsilon)
    inv_t = lax.rsqrt(sums[1] / (teacher_f.shape[1] * n_tp) + epsilon)
    normed_s = (mixed_in * inv_rms[:, None] * norm_gain[None, :]).astype(bf16)
    in_far = move(normed_s, far_pairs)
    in_near = move(normed_s, near_pairs)

    keys_part = jnp.dot(normed_s, half(w_kv, 0, 1), preferred_element_type=f32).astype(bf16)
    vals_part = jnp.dot(
        after(normed_s, teacher_got), half(w_kv, 1, 1), preferred_element_type=f32
    ).astype(bf16)
    kv_sums = [
        lax.psum_scatter(part, "tp", scatter_dimension=1, tiled=True)
        for part in (keys_part, vals_part)
    ]
    kv_sum = jnp.stack(kv_sums, axis=1)
    kv = by(s, half(kv_sum, s, 2), swap(half(kv_sum, 1 - s, 2)), 0)
    keys, vals = kv[:, 0], kv[:, 1]

    inv_t_got = swap(inv_t)

    def target_terms(position):
        rows = jnp.where(s == position, teacher_rows[0], teacher_got).astype(f32)
        inv = jnp.where(s == position, inv_t, inv_t_got)
        rows = (rows * inv[:, None] * teacher_gain[None, :]).astype(bf16)
        return lax.optimization_barrier(jnp.dot(rows, proj, preferred_element_type=f32))

    query_here, query_there = half(w_query, s, 1), half(w_query, 1 - s, 1)
    out_here, out_there = half(w_out, s, 0), half(w_out, 1 - s, 0)

    def queries(part):
        rows = across_cores(part)
        got = swap(jnp.dot(rows, query_there, preferred_element_type=f32).astype(bf16))
        own = jnp.dot(rows, query_here, preferred_element_type=f32)
        return (own + got.astype(f32)).astype(bf16)

    def output_terms(attended, target):
        got = swap(attended)
        term = jnp.dot(attended, out_here, preferred_element_type=f32)
        term = term + jnp.dot(got, out_there, preferred_element_type=f32)
        return reduce_cores(write * term - target)

    def attended_grads(grad):
        rows = across_cores(grad)
        far_term = dot_rows(rows, out_there).astype(bf16)
        got = swap(far_term)
        return (dot_rows(rows, out_here) + got.astype(f32)).astype(bf16), far_term, got

    def input_terms(grad_query):
        got = swap(grad_query)
        term = dot_rows(grad_query, query_here) + dot_rows(got, query_there)
        return reduce_cores(term).astype(bf16)

    carry = jnp.sum(hc_mix, axis=0)
    write = jnp.sum(hc_write)
    near_start = (x * length).astype(jnp.int32).reshape(1)
    far_start = ((1 - x) * length).astype(jnp.int32).reshape(1)

    query_far = queries(in_far)
    query_near = queries(in_near)
    target_far = target_terms(1 - x)
    target_near = target_terms(x)
    query_far = after(query_far, target_far)
    query_near = after(query_near, target_near)
    attended_far = attend(far_start, query_far, keys, vals)
    attended_near = attend(near_start, query_near, keys, vals)
    carried = jnp.sum(hidden * carry[None, :, None], axis=1).astype(bf16)
    carried = move(after(carried, target_far), near_pairs).astype(f32)
    term_far = output_terms(attended_far, target_far)
    term_got = chip_swap(term_far.astype(bf16))
    term_near = output_terms(attended_near, target_near)
    error = carried + term_near + term_got.astype(f32)
    loss_part = jnp.sum(error * error, axis=0, keepdims=True)
    loss_part = jnp.sum(loss_part.reshape(-1, HD), axis=0, keepdims=True)
    n_role = lax.axis_size("role")
    for axis, size in (("tp", n_tp), ("seq", n_seq), ("role", n_role)):
        step = 1
        while step < size:
            pairs = [(i, i ^ step) for i in range(size)]
            loss_part = loss_part + lax.ppermute(loss_part, axis, pairs)
            step *= 2
    loss_value = jnp.sum(loss_part) / (n_role * whole_len * features)

    grad_out = (write * error).astype(bf16)
    grad_out_far = chip_swap(grad_out)
    grad_near, near_term, near_got = attended_grads(grad_out)
    gq_near, gk_near, gv_near = attend_grad(
        near_start, query_near, keys, vals, attended_near, grad_near
    )
    grad_far = attended_grads(after(grad_out_far, near_got))[0]
    grad_far = after(grad_far, loss_value)
    base_near = move(input_terms(gq_near), near_pairs)
    gq_far, gk_far, gv_far = attend_grad(far_start, query_far, keys, vals, attended_far, grad_far)
    base_far = move(input_terms(gq_far), back_pairs)
    error_back = move(after(error.astype(bf16), near_term), near_pairs).astype(f32)

    grad_kv = jnp.stack([gk_near + gk_far, gv_near + gv_far], axis=1).astype(bf16)
    grad_kv_own = by(s, half(grad_kv, s, 0), swap(half(grad_kv, 1 - s, 0)), 2)
    grad_kv_all = lax.all_gather(grad_kv_own, "tp", axis=2, tiled=True).reshape(length, -1)
    side = dot_rows(grad_kv_all, w_kv)

    base = base_near.astype(f32) + base_far.astype(f32)
    scaled = (base + side) * norm_gain[None, :]
    inner_part = jnp.sum(scaled * mixed_in, axis=1)
    inner = lax.psum(inner_part, "tp") / features
    grad_in = inv_rms[:, None] * scaled - mixed_in * (inv_rms**3 * inner)[:, None]
    grad_streams = (
        carry[None, :, None] * error_back[:, None, :] + hc_read[None, :, None] * grad_in[:, None, :]
    )
    return (grad_streams.astype(bf16)[None], loss_value)


def solution(mesh):
    placed = (
        P("role", "seq", "tp"),
        P("tp"),
        P("tp", "seq"),
        P("role", "seq", None, "tp"),
        P(),
        P(),
        P(),
        P("tp"),
        P("seq", "tp"),
        P("tp", None),
        P("tp", "seq"),
    )
    seq, tp = mesh.shape["seq"], mesh.shape["tp"]
    by_heads = seq == 2 and tp == 4 and mesh.shape["role"] in (1, 2, 4, 8)
    return jax.shard_map(
        per_device_heads if by_heads else per_device_rows,
        mesh=mesh,
        in_specs=placed,
        out_specs=(P("role", "seq", None, "tp"), P()),
        check_vma=False,
    )
```
